512 devices in a mesh: gx: 8 (over y, core), gy: 16 (over z), gz: 4 (over x).
Axes of the slice: x: 4, y: 4, z: 16, core: 2. Of those that a mesh axis runs over, the one named last changes fastest.
Arguments:
- cotangent: float32 [3, 32, 512, 1024], P(None, 'gz', 'gy', 'gx'), may hold values from -9 to 9
- closure: int32 [2, 1024, 32], P(None, 'gx', 'gz'), may hold values from 0 to 2
- owner: int32 [1024, 512], P('gx', 'gy'), may hold values from 0 to 511, as said below
- blowing: float32 [3], replicated, may hold values from 0.5 to 2
Outputs:
- gradient: float32 [3, 32, 512, 1024], P(None, 'gz', 'gy', 'gx')
- actuator_grad: float32 [512], P(('gx', 'gy', 'gz'))
The draws below stay inside these ranges and needn't reach their ends.
Inputs may be any that keep to these rules, and one draw needn't show every extreme that they name: `owner`: the wall is cut into blocks of 32 x 32 cells aligned to multiples of those sizes; each block belongs to one actuator and each actuator owns exactly one block.
All inputs are finite; a program needn't handle non-finite values.
Results may differ from the reference program's by a relative error of at most 0.0009.
Values sent between devices are 32-bit elements; how exact they have to be, the bound alone decides.
A program may use at most 64 MiB of HBM per device.

```python
import jax
import jax.numpy as jnp
from jax import lax

CY = 32
NX = 1024
NY = 512
NZ = 32
PATCH_X = 32
ACTUATORS = 512


def draw_owner(key, part):
    patch_row = lax.broadcasted_iota(jnp.int32, (NX, NY), 0) // PATCH_X
    patch_col = lax.broadcasted_iota(jnp.int32, (NX, NY), 1) // CY
    patches = patch_row * (NY // CY) + patch_col
    ordering = jax.random.permutation(key, ACTUATORS).astype(jnp.int32)
    return ordering[patches]


def layered_field(keys, noise, y_low, y_high, x_low, x_high):
    shape = (3, NZ, NY, NX)
    y_int = lax.broadcasted_iota(jnp.int32, shape, 2)
    x_int = lax.broadcasted_iota(jnp.int32, shape, 3)
    y_pos = y_int.astype(jnp.float32)
    x_pos = x_int.astype(jnp.float32)
    y_sign = (1 - 2 * (y_int % 2)).astype(jnp.float32)
    x_sign = (1 - 2 * (x_int % 2)).astype(jnp.float32)
    y_window = jnp.sin(jnp.pi * (y_pos + 0.5) / NY) ** 2
    x_window = jnp.sin(jnp.pi * (x_pos + 0.5) / NX) ** 2
    y_flip = jnp.where(jax.random.bernoulli(keys[0], 0.5, (3, NZ, 1, NX)), 1.0, -1.0).astype(jnp.float32)
    y_size = jax.random.uniform(keys[1], (3, NZ, 1, NX), jnp.float32, y_low, y_high)
    x_flip = jnp.where(jax.random.bernoulli(keys[2], 0.5, (3, NZ, 1, 1)), 1.0, -1.0).astype(jnp.float32)
    x_size = jax.random.uniform(keys[3], (3, NZ, 1, 1), jnp.float32, x_low, x_high)
    phase = jax.random.uniform(keys[4], (3, NZ, 1, 1), jnp.float32, -jnp.pi, jnp.pi)
    y_part = y_flip * y_size * y_sign * y_window
    x_part = x_flip * x_size * x_sign * x_window * (0.75 + 0.25 * jnp.cos(2.0 * jnp.pi * y_pos / NY + phase))
    return jnp.clip(noise + y_part + x_part, -9.0, 9.0)


def draw_cotangent(key, part):
    key = jax.random.fold_in(key, 11)
    keys = jax.random.split(key, 6)
    shape = (3, NZ, NY, NX)
    noise = jnp.clip(0.4 * jax.random.normal(keys[5], shape, jnp.float32), -2.4, 2.4)
    return layered_field(keys, noise, 0.4, 0.7, 4.5, 6.5)


def with_ends(array, rng, smallest, top_value):
    longest = array.shape.index(max(array.shape))
    spots = []
    for shift in (0, 1):
        where = [jax.random.randint(jax.random.fold_in(rng, axis), (), 0, length) for axis, length in enumerate(array.shape)]
        where[longest] = (where[longest] + shift) % array.shape[longest]
        spots.append(tuple(where))
    return array.at[spots[0]].set(smallest).at[spots[1]].set(top_value)


def setup_inputs(seed: int = 0) -> dict:
    arg_keys = jax.random.split(jax.random.key(seed), 5)
    cotangent = draw_cotangent(jax.random.fold_in(arg_keys[4], 71), 0)
    closure = with_ends(jax.random.randint(arg_keys[1], (2, NX, NZ), 0, 3), jax.random.fold_in(arg_keys[1], 1), 0, 2).astype(jnp.int32)
    owner = draw_owner(jax.random.fold_in(arg_keys[4], 71), 0)
    blowing = jnp.clip(jax.random.uniform(arg_keys[3], (3,), jnp.float32, 0.5, 2.0), 0.5, 2.0)
    return dict(cotangent=cotangent, closure=closure, owner=owner, blowing=blowing)


deriv_alpha = 1.0 / 3.0
deriv_near = 14.0 / 9.0
deriv_far = 1.0 / 9.0
filter_alpha = 0.499
filter_coefs = [(193.0 + 126.0 * filter_alpha) / 256.0, (105.0 + 302.0 * filter_alpha) / 256.0, 15.0 * (2.0 * filter_alpha - 1.0) / 64.0, 45.0 * (1.0 - 2.0 * filter_alpha) / 512.0, 5.0 * (2.0 * filter_alpha - 1.0) / 256.0, (1.0 - 2.0 * filter_alpha) / 512.0]

def reference(cotangent, closure, owner, blowing):
    fields, count_z, count_y, count_x = cotangent.shape
    number_type = cotangent.dtype
    coupling = jnp.transpose(0.5 * filter_alpha * closure.astype(number_type), (0, 2, 1))
    line_shape = (count_z, count_x, count_y)
    below_diag = jnp.full(line_shape, filter_alpha, number_type).at[:, :, 0].set(0.0).at[:, :, 1].set(coupling[0])
    above_diag = jnp.full(line_shape, filter_alpha, number_type).at[:, :, count_y - 2].set(coupling[1]).at[:, :, count_y - 1].set(0.0)
    main_diag = jnp.ones(line_shape, number_type)
    below_x = jnp.full((count_x,), deriv_alpha, number_type).at[0].set(0.0)
    above_x = jnp.full((count_x,), deriv_alpha, number_type).at[count_x - 1].set(0.0)
    main_x = jnp.ones((count_x,), number_type)

    def one_field(field):
        lines = jnp.transpose(field, (0, 2, 1))
        solved = lax.linalg.tridiagonal_solve(below_diag, main_diag, above_diag, lines[..., None])[..., 0]
        padded = jnp.pad(solved, ((0, 0), (0, 0), (5, 5)))
        filtered = filter_coefs[0] * solved
        for reach_cells in range(1, 6):
            filtered = filtered + 0.5 * filter_coefs[reach_cells] * (padded[..., 5 + reach_cells:5 + reach_cells + count_y] + padded[..., 5 - reach_cells:5 - reach_cells + count_y])
        filtered = jnp.transpose(filtered, (0, 2, 1))
        columns = filtered.reshape(-1, count_x).T
        potential = lax.linalg.tridiagonal_solve(below_x, main_x, above_x, columns).T.reshape(count_z, count_y, count_x)
        rimmed = jnp.pad(potential, ((0, 0), (0, 0), (2, 2)))
        return -(0.5 * deriv_near * (rimmed[..., 3:3 + count_x] - rimmed[..., 1:1 + count_x]) + 0.25 * deriv_far * (rimmed[..., 4:4 + count_x] - rimmed[..., 0:count_x]))
    gradient = lax.map(one_field, cotangent)
    surface = jnp.sum(blowing[:, None, None] * gradient[:, 0, :, :], axis=0)
    actuator_grad = jax.ops.segment_sum(surface.T.reshape(-1), owner.reshape(-1), num_segments=ACTUATORS)
    return (gradient, actuator_grad)
```

```python
import functools

import numpy as np

import jax
import jax.numpy as jnp
from jax import lax
from jax.experimental import pallas as pl
from jax.experimental.pallas import tpu as pltpu
from jax.sharding import PartitionSpec as P

MESH = pl.DeviceIdType.MESH
F32 = jnp.float32
ALPHA = 0.499
COEFS = [
    (193.0 + 126.0 * ALPHA) / 256.0,
    (105.0 + 302.0 * ALPHA) / 256.0,
    15.0 * (2.0 * ALPHA - 1.0) / 64.0,
    45.0 * (1.0 - 2.0 * ALPHA) / 512.0,
    5.0 * (2.0 * ALPHA - 1.0) / 256.0,
    (1.0 - 2.0 * ALPHA) / 512.0,
]
PATCH = 32
SOLVERS = 3


def toeplitz(size, offsets):
    out = np.zeros((size, size))
    for offset, value in offsets.items():
        out += np.diag(np.full(size - abs(offset), value), offset)
    return out


def constants(gx, gy, ny, nx, nz):
    c = {}
    big_y, big_x = gy * ny, gx * nx
    root = (-1.0 + np.sqrt(1.0 - 4.0 * ALPHA**2)) / (2.0 * ALPHA)
    amp = 1.0 / np.sqrt(1.0 - 4.0 * ALPHA**2)
    half = {n: (COEFS[0] if n == 0 else 0.5 * COEFS[n]) for n in range(6)}
    stencil = np.array([half[abs(n)] for n in range(-5, 6)])
    quotient = np.zeros(11)
    rest = stencil.copy()
    for n in range(5, 0, -1):
        q = rest[5 + n] / ALPHA
        for m in {n - 1, 1 - n}:
            quotient[5 + m] += q if m else q
            rest[5 + m - 1 : 5 + m + 2] -= q * np.array([ALPHA, 1.0, ALPHA])
    lam = rest[5]
    cq = {d: quotient[5 + d] for d in range(-4, 5)}
    t_local = np.linalg.inv(toeplitz(ny, {-1: ALPHA, 0: 1.0, 1: ALPHA}))
    inner = toeplitz(ny, cq) + lam * t_local
    c["inner"] = np.kron(np.eye(nz), inner)
    j = np.arange(ny)
    c["pq"] = np.concatenate(
        [np.kron(np.eye(nz), root ** (ny - 1 - j)[None]), np.kron(np.eye(nz), root**j[None])]
    )
    kinds = np.zeros((3, ny, 12))
    for kind in range(3):
        for h in range(4):
            for row in range(ny):
                low, high = h - 4 - row, ny + h - row
                if kind > 0 and abs(low) <= 4:
                    kinds[kind, row, h] = cq[low]
                if kind < 2 and abs(high) <= 4:
                    kinds[kind, row, 4 + h] = cq[high]
        kinds[kind, :, 8] = -lam * ALPHA * t_local[:, 0]
        kinds[kind, :, 9] = -lam * ALPHA * t_local[:, -1]
    edge = np.array([cq[-1 - row] if row < 4 else 0.0 for row in range(ny)])
    kinds[0, :, 8] = ALPHA * edge
    kinds[0, :, 10] = inner[:, 1]
    kinds[2, :, 9] = ALPHA * edge[::-1]
    kinds[2, :, 11] = inner[:, ny - 2]
    c["sides"] = np.stack(
        [np.einsum("ri,zw->zriw", k, np.eye(nz)).reshape(nz * ny, 12 * nz) for k in kinds]
    )
    t_inv = np.linalg.inv(toeplitz(big_y, {-1: ALPHA, 0: 1.0, 1: ALPHA}))
    c["t_inv"], c["root"], c["amp"] = t_inv, root, amp
    third = 1.0 / 3.0
    s = (-1.0 + np.sqrt(1.0 - 4.0 * third**2)) / (2.0 * third)
    amp_x = 1.0 / np.sqrt(1.0 - 4.0 * third**2)
    q_mat = toeplitz(big_x, {1: 7.0 / 9.0, -1: -7.0 / 9.0, 2: 1.0 / 36.0, -2: -1.0 / 36.0})
    p_mat = toeplitz(big_x, {-1: third, 0: 1.0, 1: third})
    d_mat = -np.linalg.solve(p_mat, q_mat.T).T
    c["d_mat"] = d_mat
    c["local"] = np.stack([d_mat[k * nx : (k + 1) * nx, k * nx : (k + 1) * nx].T for k in range(gx)])
    x = np.arange(nx)
    fun = np.zeros((4, nx))
    fun[0], fun[1] = s ** (nx - 1 - x), s**x
    fun[2, 0], fun[3, nx - 1] = 1.0, 1.0
    c["fun"] = np.repeat(fun.T, ny, axis=1)
    c["val"] = np.stack(
        [np.einsum("ri,fx->ixfr", k[:, 8:], fun).reshape(4 * nx, 4 * ny) for k in kinds]
    )
    i = np.arange(-1, nx + 1)
    shape_s, shape_r = amp_x * s ** (i + 1), amp_x * s ** (nx - i)
    shapes = np.zeros((gx, 4, nx))
    for k in range(gx):
        for f, w in ((0, shape_s), (1, shape_r)):
            shapes[k, f] = -25.0 / 36.0 * (w[2:] - w[:-2])
            if k == 0:
                shapes[k, f, 0] += w[1] / 36.0
            if k == gx - 1:
                shapes[k, f, -1] -= w[nx] / 36.0
        shapes[k, 3, 0], shapes[k, 2, -1] = 1.0 / 12.0, -1.0 / 12.0
    c["shapes"] = np.repeat(shapes, ny, axis=1)
    mix = np.zeros((gx, gx, 4, 4))
    norm = 1.0 / (1.0 - s ** (2.0 * (big_x + 1)))
    for k in range(gx):
        for m in range(gx):
            k0, m0 = k * nx, m * nx
            m1 = m0 + nx - 1
            if m < k:
                mix[k, m, 0, 0] = norm * s ** float(k0 - m1 - 1)
                mix[k, m, 0, 1] = norm * s ** float(2 * big_x + 2 - nx - k0 + m0)
            if m > k:
                mix[k, m, 0, 1] = norm * s ** float(m0 - k0 - nx)
                mix[k, m, 0, 0] = norm * s ** float(2 * big_x + 1 + k0 - m1)
            if m != k:
                mix[k, m, 1, 0] = -norm * s ** float(2 * big_x - k0 - nx - m1)
                mix[k, m, 2, 1] = -norm * s ** float(k0 + m0 + 1)
            mix[k, m, 0, 2], mix[k, m, 0, 3] = float(m == k + 1), float(m == k - 1)
    c["mix"] = np.repeat(mix, ny, axis=3)
    b_mat = toeplitz(big_y, {n: half[abs(n)] for n in range(-5, 6)})
    col_sums = (b_mat @ t_inv).reshape(gy, ny, big_y).sum(1)
    groups = gy // 4
    wall = np.zeros((gy, 4, 8, ny))
    for m in range(gy):
        rows = col_sums[:, m * ny : (m + 1) * ny]
        for y in range(gy):
            wall[m, y % 4, y // 4] = rows[y]
        wall[m, 0, 4] = t_inv[0, m * ny : (m + 1) * ny]
        wall[m, 0, 5] = t_inv[-1, m * ny : (m + 1) * ny]
    assert groups <= 4
    c["wall"] = wall.reshape(gy, 32, ny)
    ends = np.zeros((2, 4, 8))
    for y in range(gy):
        ends[0, y % 4, y // 4], ends[1, y % 4, y // 4] = col_sums[y, 1], col_sums[y, -2]
    c["ends"] = np.repeat(ends.reshape(2, 32, 1), 128, axis=2)
    patch = np.zeros((gx, nx, 4, 32))
    sums = d_mat.reshape(big_x // PATCH, PATCH, big_x).sum(1)
    for k in range(gx):
        patch[k, :, :, : sums.shape[0]] = sums[:, k * nx : (k + 1) * nx].T[:, None, :]
    c["patch"] = patch.reshape(gx, nx, 128)
    return c


def dot(a, b):
    return jnp.dot(a, b, preferred_element_type=F32, precision=lax.Precision.HIGHEST)


def kernel(
    sizes, cst,
    cot_h, closure_h, owner_h, blow_h,
    inner_h, pq_h, sides_h, fun_h, val_h, local_h, shapes_h, mix_h, wall_h, ends_h, patch_h,
    grad_o, act_o,
    cot, closure, owner, blow, inner, pq, sides, fun, val, local, shapes, mix, wall, ends, patch,
    pq_out, pq_in, halo_out, halo_in, v_out, v_in, w_out, w_in, tot_out, tot_in, x_out, x_in,
    load_sem, send_sem, recv_sem, v_sem,
):
    gx_n, gy_n, gz_n, ny, nx, nz = sizes
    gx, gy, gz = (lax.axis_index(a) for a in ("gx", "gy", "gz"))
    big_y = gy_n * ny
    planes = 3 * nz

    barrier = pltpu.get_barrier_semaphore()

    def greet(**where):
        pl.semaphore_signal(barrier, inc=1, device_id=where, device_id_type=MESH)

    def load(k, src, dst):
        copy = pltpu.make_async_copy(src, dst, load_sem.at[k])
        copy.start()
        return copy

    first = [load(0, cot_h, cot), load(1, pq_h, pq)]
    for d in range(1, gx_n):
        greet(gx=lax.rem(gx + d, gx_n))
    for d in (1, gy_n - 1):
        greet(gy=lax.rem(gy + d, gy_n))

    @pl.when(gy < SOLVERS)
    def _():
        for d in range(1, gy_n):
            greet(gy=lax.rem(gy + d, gy_n))

    @pl.when(gy == 0)
    def _():
        for d in range(1, gy_n):
            greet(gy=lax.rem(gy + d, gy_n), gz=0)

        @pl.when(gz != 0)
        def _():
            greet(gz=0)

    kind = jnp.where(gy == 0, 0, jnp.where(gy == gy_n - 1, 2, 1))
    rest = [
        load(2, closure_h, closure), load(3, owner_h, owner), load(4, wall_h.at[gy], wall),
        load(5, ends_h, ends), load(6, patch_h.at[gx], patch), load(7, inner_h, inner),
        load(8, sides_h.at[kind], sides), load(9, fun_h, fun), load(10, val_h.at[kind], val),
        load(11, local_h.at[gx], local), load(12, shapes_h.at[gx], shapes), load(13, mix_h.at[gx], mix),
        load(14, blow_h, blow),
    ]

    for copy in first:
        copy.wait()
    for c in range(3):
        pair = dot(pq[...], cot[c * nz * ny : (c + 1) * nz * ny, :])
        pq_out[c, 0] = pair[:nz]
        pq_out[c, 1] = pair[nz:]

    n_wait = (gx_n - 1) + 2 + SOLVERS - (gy < SOLVERS).astype(jnp.int32)
    n_wait += jnp.where(gz == 0, gz_n - (gy == 0).astype(jnp.int32), 0)
    pl.semaphore_wait(barrier, n_wait)

    def pq_copy(c):
        return pltpu.make_async_remote_copy(
            src_ref=pq_out.at[c], dst_ref=pq_in.at[gy], send_sem=send_sem.at[c], recv_sem=recv_sem.at[0],
            device_id={"gy": c}, device_id_type=MESH)

    for c in range(SOLVERS):
        @pl.when(gy != c)
        def _():
            pq_copy(c).start()

        @pl.when(gy == c)
        def _():
            pq_in[gy] = pq_out[c]

    for r in range(4):
        for c in range(3):
            base = c * nz * ny
            halo_out[0, r, c * nz : (c + 1) * nz] = cot[pl.ds(base + ny - 4 + r, nz, stride=ny), :]
            halo_out[1, r, c * nz : (c + 1) * nz] = cot[pl.ds(base + r, nz, stride=ny), :]

    def halo_copy(side):
        return pltpu.make_async_remote_copy(
            src_ref=halo_out.at[side], dst_ref=halo_in.at[side], send_sem=send_sem.at[3 + side],
            recv_sem=recv_sem.at[1 + side],
            device_id={"gy": lax.rem(gy + (1 if side == 0 else gy_n - 1), gy_n)}, device_id_type=MESH)

    for side in (0, 1):
        halo_copy(side).start()

    for copy in rest:
        copy.wait()
    deltas = []
    for side in (0, 1):
        deltas.append(ALPHA - (0.5 * ALPHA) * closure[side].astype(F32))
    delta0, delta1 = deltas
    tau, eps = float(cst["t_inv"][0, 1]), float(cst["t_inv"][0, big_y - 2])

    def ends_of(y0, y1, d0, d1):
        p0, p1 = 1.0 - tau * d0, 1.0 - tau * d1
        scale = 1.0 / (p0 * p1 - (eps * eps) * (d0 * d1))
        return (p1 * y0 + eps * (d1 * y1)) * scale, (p0 * y1 + eps * (d0 * y0)) * scale

    lane = lax.broadcasted_iota(jnp.int32, (8, 128), 1)
    row = lax.broadcasted_iota(jnp.int32, (8, 128), 0)

    def wall_copy(z):
        return pltpu.make_async_remote_copy(
            src_ref=w_out, dst_ref=w_in.at[gy], send_sem=send_sem.at[5 + z], recv_sem=recv_sem.at[3],
            device_id={"gy": 0, "gz": z}, device_id_type=MESH)

    @pl.when(gz == 0)
    def _():
        blend = sum(blow[c] * cot[c * nz * ny : c * nz * ny + ny, :] for c in range(3))
        parts = dot(wall[...], blend)
        x0, x1 = ends_of(parts[4:5], parts[5:6], delta0[0:1], delta1[0:1])
        parts = parts + ends[0] * (delta0[0:1] * x0) + ends[1] * (delta1[0:1] * x1)
        spread = dot(parts, patch[...])
        total = jnp.zeros((8, 128), F32)
        for q in range(4):
            total += jnp.where((lane // 32 == q) & (row < 4), spread[8 * q : 8 * q + 8], 0.0)
        at = (row == 4 + gy // 4) & (lane // 32 == lax.rem(gy, 4))
        for q in range(nx // PATCH):
            owned = owner[0:1, q * PATCH : q * PATCH + 1].astype(F32)
            total += jnp.where(at & (lane % 32 == gx * (nx // PATCH) + q), owned, 0.0)
        w_out[...] = total
        for z in range(gz_n):
            if z == 0:
                @pl.when(gy != 0)
                def _():
                    wall_copy(0).start()

                @pl.when(gy == 0)
                def _():
                    w_in[0] = w_out[...]
            else:
                wall_copy(z).start()

    u = [dot(inner[...], cot[c * nz * ny : (c + 1) * nz * ny, :]) for c in range(3)]
    for c in range(3):
        grad_o[c * nz * ny : (c + 1) * nz * ny, :] = u[c]

    def v_copy(c, k):
        return pltpu.make_async_remote_copy(
            src_ref=v_out.at[k], dst_ref=v_in.at[c], send_sem=send_sem.at[9], recv_sem=v_sem.at[c],
            device_id={"gy": k}, device_id_type=MESH)

    root, amp, t_inv = cst["root"], cst["amp"], cst["t_inv"]

    @pl.when(gy < SOLVERS)
    def _():
        pltpu.make_async_remote_copy(
            src_ref=pq_in.at[0 : gy_n - 1], dst_ref=pq_in.at[0 : gy_n - 1], send_sem=send_sem.at[0],
            recv_sem=recv_sem.at[0], device_id={"gy": 0}, device_id_type=MESH).wait_recv()
        hop = float(root**ny)
        before, after = [None] * gy_n, [None] * gy_n
        run = jnp.zeros((nz, nx), F32)
        for m in range(gy_n):
            before[m] = run
            run = hop * run + pq_in[m, 0]
        p_all = run
        run = jnp.zeros((nz, nx), F32)
        for m in reversed(range(gy_n)):
            after[m] = run
            run = hop * run + pq_in[m, 1]
        q_all = run
        far = float(root ** (big_y + 1))
        norm = -amp / (1.0 - far * far)
        a = float(norm * root) * (q_all - far * p_all)
        b = float(norm * root) * (p_all - far * q_all)
        y0 = float(amp) * q_all + float(root) * a + float(root**big_y) * b
        y1 = float(amp) * p_all + float(root**big_y) * a + float(root) * b
        x0, x1 = ends_of(y0, y1, delta0, delta1)
        w0, w1 = delta0 * x0, delta1 * x1

        def at(i, value):
            value = float(amp) * value + float(root ** (i + 1)) * a + float(root ** (big_y - i)) * b
            return value + float(t_inv[i, 1]) * w0 + float(t_inv[i, big_y - 2]) * w1

        for k in range(gy_n):
            if k == 0:
                v_out[k, 0] = x0
            else:
                v_out[k, 0] = at(k * ny - 1, before[k] + float(root) * (hop * after[k] + pq_in[k, 1]))
            if k == gy_n - 1:
                v_out[k, 1] = x1
            else:
                v_out[k, 1] = at((k + 1) * ny, float(root) * (hop * before[k] + pq_in[k, 0]) + after[k])
            for c in range(SOLVERS):
                if c == k:
                    @pl.when(gy == c)
                    def _():
                        v_in[c] = v_out[k]
                else:
                    @pl.when(gy == c)
                    def _():
                        v_copy(c, k).start()

    def tot_copy(k):
        return pltpu.make_async_remote_copy(
            src_ref=tot_out, dst_ref=tot_in, send_sem=send_sem.at[10], recv_sem=recv_sem.at[4],
            device_id={"gy": k}, device_id_type=MESH)

    @pl.when(gy == 0)
    def _():
        @pl.when(gz == 0)
        def _():
            pltpu.make_async_remote_copy(
                src_ref=w_in.at[1:gy_n], dst_ref=w_in.at[1:gy_n], send_sem=send_sem.at[5],
                recv_sem=recv_sem.at[3], device_id={"gy": 0}, device_id_type=MESH).wait_recv()

        @pl.when(gz != 0)
        def _():
            pltpu.make_async_remote_copy(
                src_ref=w_in, dst_ref=w_in, send_sem=send_sem.at[5],
                recv_sem=recv_sem.at[3], device_id={"gy": 0}, device_id_type=MESH).wait_recv()
        total = w_in[0]
        for m in range(1, gy_n):
            total = total + w_in[m]
        tot_out[...] = total
        tot_in[...] = total
        for k in range(1, gy_n):
            tot_copy(k).start()

    for side in (0, 1):
        halo_copy(side).wait_recv()
    same_row = (
        lax.broadcasted_iota(jnp.int32, (nz * ny, 128), 0) % ny
        == lax.broadcasted_iota(jnp.int32, (nz * ny, 128), 1) % ny
    )
    plane_of = (
        lax.broadcasted_iota(jnp.int32, (nz, nz * ny), 1) // ny
        == lax.broadcasted_iota(jnp.int32, (nz, nz * ny), 0)
    ).astype(F32)
    x0_parts = []
    for c in range(3):
        rows = halo_in[:, :, c * nz : (c + 1) * nz, :].reshape(8 * nz, nx)
        u_c = grad_o[c * nz * ny : (c + 1) * nz * ny, :] + dot(sides[:, : 8 * nz], rows)
        grad_o[c * nz * ny : (c + 1) * nz * ny, :] = u_c
        x0_parts.append(dot(plane_of, jnp.where(same_row, dot(u_c, fun[...]), 0.0)))

    for c in range(SOLVERS):
        @pl.when(gy != c)
        def _():
            v_copy(c, 0).wait_recv()

    v_rows = []
    for c in range(3):
        low, high = v_in[c, 0], v_in[c, 1]
        v_rows.append([low, high, delta0 * low, delta1 * high])
        x_out[c * nz : (c + 1) * nz] = x0_parts[c] + dot(jnp.concatenate(v_rows[c], axis=1), val[...])

    @pl.when(gy != 0)
    def _():
        tot_copy(0).wait_recv()

    x_out[planes : planes + 8] = tot_in[...]

    def x_copy(d):
        return pltpu.make_async_remote_copy(
            src_ref=x_out, dst_ref=x_in.at[gx], send_sem=send_sem.at[11], recv_sem=recv_sem.at[5],
            device_id={"gx": lax.rem(gx + d, gx_n)}, device_id_type=MESH)

    for d in range(1, gx_n):
        x_copy(d).start()
    x_in[gx] = x_out[...]

    for c in range(3):
        u_c = grad_o[c * nz * ny : (c + 1) * nz * ny, :] + dot(
            sides[:, 8 * nz :], jnp.concatenate(v_rows[c], axis=0))
        grad_o[c * nz * ny : (c + 1) * nz * ny, :] = dot(u_c, local[...])

    pltpu.make_async_remote_copy(
        src_ref=x_in.at[0 : gx_n - 1], dst_ref=x_in.at[0 : gx_n - 1], send_sem=send_sem.at[11],
        recv_sem=recv_sem.at[5], device_id={"gx": 0}, device_id_type=MESH).wait_recv()
    for c in range(3):
        value, to_r, to_p = (jnp.zeros((nz, 128), F32) for _ in range(3))
        for m in range(gx_n):
            part = x_in[m, c * nz : (c + 1) * nz]
            value += mix[m, 0:1] * part
            to_r += mix[m, 1:2] * part
            to_p += mix[m, 2:3] * part
        value += pltpu.roll(to_r, ny, 1) + pltpu.roll(to_p, 128 - ny, 1)
        spread = jnp.broadcast_to(value[:, None, :], (nz, ny, 128)).reshape(nz * ny, 128)
        spread = jnp.where(same_row, spread, 0.0)
        grad_o[c * nz * ny : (c + 1) * nz * ny, :] += dot(spread, shapes[...])
    total = x_in[0, planes : planes + 8]
    for m in range(1, gx_n):
        total = total + x_in[m, planes : planes + 8]
    mine = ((gx * gy_n + gy) * gz_n + gz).astype(F32)
    hit = (pltpu.roll(total, 4, 0) == mine) & (row < gy_n // 4) & (lane % 32 < gx_n * nx // PATCH)
    act_o[...] = jnp.sum(jnp.where(hit, total, 0.0), keepdims=True)

    for c in range(SOLVERS):
        @pl.when(gy != c)
        def _():
            pq_copy(c).wait_send()
    for side in (0, 1):
        halo_copy(side).wait_send()

    @pl.when(gz == 0)
    def _():
        for z in range(1, gz_n):
            wall_copy(z).wait_send()

        @pl.when(gy != 0)
        def _():
            wall_copy(0).wait_send()

    @pl.when(gy < SOLVERS)
    def _():
        pltpu.make_async_remote_copy(
            src_ref=v_out.at[0 : gy_n - 1], dst_ref=v_out.at[0 : gy_n - 1], send_sem=send_sem.at[9],
            recv_sem=v_sem.at[0], device_id={"gy": 0}, device_id_type=MESH).wait_send()

    @pl.when(gy == 0)
    def _():
        for k in range(1, gy_n):
            tot_copy(k).wait_send()

    for d in range(1, gx_n):
        x_copy(d).wait_send()


def on_device(sizes, cst, cotangent, closure, owner, blowing):
    gx_n, gy_n, gz_n, ny, nx, nz = sizes
    f32 = lambda name: jnp.asarray(np.asarray(cst[name], np.float32))
    tables = [f32(n) for n in ("inner", "pq", "sides", "fun", "val", "local", "shapes", "mix", "wall", "ends", "patch")]
    anyspec = pl.BlockSpec(memory_space=pltpu.HBM)
    vmem = pl.BlockSpec(memory_space=pltpu.VMEM)
    v = lambda *shape: pltpu.VMEM(shape, F32)
    rows = 3 * nz * ny
    scratch = [
        v(rows, nx), pltpu.VMEM((2, nz, nx), jnp.int32), pltpu.VMEM((ny, nx), jnp.int32), pltpu.SMEM((3,), F32),
        v(nz * ny, nz * ny), v(2 * nz, nz * ny), v(nz * ny, 12 * nz), v(nx, 128), v(4 * nx, 128),
        v(nx, nx), v(128, nx), v(gx_n, 4, 128), v(32, ny), v(2, 32, 128), v(nx, 128),
        v(3, 2, nz, nx), v(gy_n, 2, nz, nx), v(2, 4, 3 * nz, nx), v(2, 4, 3 * nz, nx),
        v(gy_n, 2, nz, nx), v(3, 2, nz, nx), v(8, 128), v(gy_n, 8, 128), v(8, 128), v(8, 128),
        v(3 * nz + 8, 128), v(gx_n, 3 * nz + 8, 128),
        pltpu.SemaphoreType.DMA((15,)), pltpu.SemaphoreType.DMA((12,)), pltpu.SemaphoreType.DMA((6,)),
        pltpu.SemaphoreType.DMA((3,)),
    ]
    gradient, share = pl.pallas_call(
        functools.partial(kernel, sizes, cst),
        out_shape=(jax.ShapeDtypeStruct((rows, nx), F32), jax.ShapeDtypeStruct((1, 1), F32)),
        in_specs=[anyspec] * (4 + len(tables)),
        out_specs=(vmem, vmem),
        scratch_shapes=scratch,
        compiler_params=pltpu.CompilerParams(
            collective_id=0, has_side_effects=True, vmem_limit_bytes=64 * 1024 * 1024
        ),
    )(cotangent.reshape(rows, nx), jnp.transpose(closure, (0, 2, 1)), owner.T, blowing, *tables)
    return gradient.reshape(cotangent.shape), share.reshape(1)


def solution(mesh):
    gx_n, gy_n, gz_n = (mesh.shape[a] for a in ("gx", "gy", "gz"))
    sizes = (gx_n, gy_n, gz_n, 512 // 16, 1024 // 8, 32 // 4)
    cst = constants(gx_n, gy_n, sizes[3], sizes[4], sizes[5])
    in_specs = (P(None, "gz", "gy", "gx"), P(None, "gx", "gz"), P("gx", "gy"), P())
    out_specs = (P(None, "gz", "gy", "gx"), P(("gx", "gy", "gz")))
    return jax.shard_map(
        functools.partial(on_device, sizes, cst),
        mesh=mesh, in_specs=in_specs, out_specs=out_specs, check_vma=False,
    )
```

```python
import functools

import numpy as np

import jax
import jax.numpy as jnp
from jax import lax
from jax.experimental import pallas as pl
from jax.experimental.pallas import tpu as pltpu
from jax.sharding import PartitionSpec as P

MESH = pl.DeviceIdType.MESH
F32 = jnp.float32
ALPHA = 0.499
COEFS = [
    (193.0 + 126.0 * ALPHA) / 256.0,
    (105.0 + 302.0 * ALPHA) / 256.0,
    15.0 * (2.0 * ALPHA - 1.0) / 64.0,
    45.0 * (1.0 - 2.0 * ALPHA) / 512.0,
    5.0 * (2.0 * ALPHA - 1.0) / 256.0,
    (1.0 - 2.0 * ALPHA) / 512.0,
]
PATCH = 32


def toeplitz(size, offsets):
    out = np.zeros((size, size))
    for offset, value in offsets.items():
        out += np.diag(np.full(size - abs(offset), value), offset)
    return out


def constants(gx, gy, ny, nx, nz):
    c = {}
    big_y, big_x = gy * ny, gx * nx
    root = (-1.0 + np.sqrt(1.0 - 4.0 * ALPHA**2)) / (2.0 * ALPHA)
    amp = 1.0 / np.sqrt(1.0 - 4.0 * ALPHA**2)
    half = {n: (COEFS[0] if n == 0 else 0.5 * COEFS[n]) for n in range(6)}
    stencil = np.array([half[abs(n)] for n in range(-5, 6)])
    quotient = np.zeros(11)
    rest = stencil.copy()
    for n in range(5, 0, -1):
        q = rest[5 + n] / ALPHA
        for m in {n - 1, 1 - n}:
            quotient[5 + m] += q if m else q
            rest[5 + m - 1 : 5 + m + 2] -= q * np.array([ALPHA, 1.0, ALPHA])
    lam = rest[5]
    cq = {d: quotient[5 + d] for d in range(-4, 5)}
    t_local = np.linalg.inv(toeplitz(ny, {-1: ALPHA, 0: 1.0, 1: ALPHA}))
    inner = toeplitz(ny, cq) + lam * t_local
    c["inner"] = np.kron(np.eye(nz), inner)
    j = np.arange(ny)
    c["pq"] = np.concatenate(
        [np.kron(np.eye(nz), root ** (ny - 1 - j)[None]), np.kron(np.eye(nz), root**j[None])]
    )
    kinds = np.zeros((3, ny, 12))
    for kind in range(3):
        for h in range(4):
            for row in range(ny):
                low, high = h - 4 - row, ny + h - row
                if kind > 0 and abs(low) <= 4:
                    kinds[kind, row, h] = cq[low]
                if kind < 2 and abs(high) <= 4:
                    kinds[kind, row, 4 + h] = cq[high]
        kinds[kind, :, 8] = -lam * ALPHA * t_local[:, 0]
        kinds[kind, :, 9] = -lam * ALPHA * t_local[:, -1]
    edge = np.array([cq[-1 - row] if row < 4 else 0.0 for row in range(ny)])
    kinds[0, :, 8] = ALPHA * edge
    kinds[0, :, 10] = inner[:, 1]
    kinds[2, :, 9] = ALPHA * edge[::-1]
    kinds[2, :, 11] = inner[:, ny - 2]
    c["sides"] = np.stack(
        [np.einsum("ri,zw->zriw", k, np.eye(nz)).reshape(nz * ny, 12 * nz) for k in kinds]
    )
    t_inv = np.linalg.inv(toeplitz(big_y, {-1: ALPHA, 0: 1.0, 1: ALPHA}))
    c["t_inv"], c["root"], c["amp"] = t_inv, root, amp
    third = 1.0 / 3.0
    s = (-1.0 + np.sqrt(1.0 - 4.0 * third**2)) / (2.0 * third)
    amp_x = 1.0 / np.sqrt(1.0 - 4.0 * third**2)
    q_mat = toeplitz(big_x, {1: 7.0 / 9.0, -1: -7.0 / 9.0, 2: 1.0 / 36.0, -2: -1.0 / 36.0})
    p_mat = toeplitz(big_x, {-1: third, 0: 1.0, 1: third})
    d_mat = -np.linalg.solve(p_mat, q_mat.T).T
    c["d_mat"] = d_mat
    c["local"] = np.stack([d_mat[k * nx : (k + 1) * nx, k * nx : (k + 1) * nx].T for k in range(gx)])
    x = np.arange(nx)
    fun = np.zeros((4, nx))
    fun[0], fun[1] = s ** (nx - 1 - x), s**x
    fun[2, 0], fun[3, nx - 1] = 1.0, 1.0
    c["fun"] = np.repeat(fun.T, ny, axis=1)
    c["val"] = np.stack(
        [np.einsum("ri,fx->ixfr", k[:, 8:], fun).reshape(4 * nx, 4 * ny) for k in kinds]
    )
    i = np.arange(-1, nx + 1)
    shape_s, shape_r = amp_x * s ** (i + 1), amp_x * s ** (nx - i)
    shapes = np.zeros((gx, 4, nx))
    for k in range(gx):
        for f, w in ((0, shape_s), (1, shape_r)):
            shapes[k, f] = -25.0 / 36.0 * (w[2:] - w[:-2])
            if k == 0:
                shapes[k, f, 0] += w[1] / 36.0
            if k == gx - 1:
                shapes[k, f, -1] -= w[nx] / 36.0
        shapes[k, 3, 0], shapes[k, 2, -1] = 1.0 / 12.0, -1.0 / 12.0
    c["shapes"] = np.repeat(shapes, ny, axis=1)
    mix = np.zeros((gx, gx, 4, 4))
    norm = 1.0 / (1.0 - s ** (2.0 * (big_x + 1)))
    for k in range(gx):
        for m in range(gx):
            k0, m0 = k * nx, m * nx
            m1 = m0 + nx - 1
            if m < k:
                mix[k, m, 0, 0] = norm * s ** float(k0 - m1 - 1)
                mix[k, m, 0, 1] = norm * s ** float(2 * big_x + 2 - nx - k0 + m0)
            if m > k:
                mix[k, m, 0, 1] = norm * s ** float(m0 - k0 - nx)
                mix[k, m, 0, 0] = norm * s ** float(2 * big_x + 1 + k0 - m1)
            if m != k:
                mix[k, m, 1, 0] = -norm * s ** float(2 * big_x - k0 - nx - m1)
                mix[k, m, 2, 1] = -norm * s ** float(k0 + m0 + 1)
            mix[k, m, 0, 2], mix[k, m, 0, 3] = float(m == k + 1), float(m == k - 1)
    c["mix"] = np.repeat(mix, ny, axis=3)
    b_mat = toeplitz(big_y, {n: half[abs(n)] for n in range(-5, 6)})
    col_sums = (b_mat @ t_inv).reshape(gy, ny, big_y).sum(1)
    groups = gy // 4
    wall = np.zeros((gy, 4, 8, ny))
    for m in range(gy):
        rows = col_sums[:, m * ny : (m + 1) * ny]
        for y in range(gy):
            wall[m, y % 4, y // 4] = rows[y]
        wall[m, 0, 4] = t_inv[0, m * ny : (m + 1) * ny]
        wall[m, 0, 5] = t_inv[-1, m * ny : (m + 1) * ny]
    assert groups <= 4
    c["wall"] = wall.reshape(gy, 32, ny)
    ends = np.zeros((2, 4, 8))
    for y in range(gy):
        ends[0, y % 4, y // 4], ends[1, y % 4, y // 4] = col_sums[y, 1], col_sums[y, -2]
    c["ends"] = np.repeat(ends.reshape(2, 32, 1), 128, axis=2)
    patch = np.zeros((gx, nx, 4, 32))
    sums = d_mat.reshape(big_x // PATCH, PATCH, big_x).sum(1)
    for k in range(gx):
        patch[k, :, :, : sums.shape[0]] = sums[:, k * nx : (k + 1) * nx].T[:, None, :]
    c["patch"] = patch.reshape(gx, nx, 128)
    return c


def dot(a, b):
    return jnp.dot(a, b, preferred_element_type=F32, precision=lax.Precision.HIGHEST)


def kernel(
    sizes, cst,
    cot_h, closure_h, owner_h, blow_h,
    inner_h, pq_h, sides_h, fun_h, val_h, local_h, mix_h, wall_h, ends_h, patch_h,
    grad_o, small_o,
    cot, closure, owner, blow, inner, pq, sides, fun, val, local, mix, wall, ends, patch,
    pq_out, pq_in, halo_out, halo_in, v_out, v_in, w_out, w_in, tot_out, tot_in, x_out, x_in, sum_in, own,
    load_sem, send_sem, recv_sem,
):
    gx_n, gy_n, gz_n, ny, nx, nz = sizes
    gx, gy, gz = (lax.axis_index(a) for a in ("gx", "gy", "gz"))
    big_y = gy_n * ny
    planes = 3 * nz

    barrier = pltpu.get_barrier_semaphore()

    def greet(**where):
        pl.semaphore_signal(barrier, inc=1, device_id=where, device_id_type=MESH)

    def load(k, src, dst):
        copy = pltpu.make_async_copy(src, dst, load_sem.at[k])
        copy.start()
        return copy

    first = [load(0, cot_h, cot), load(1, pq_h, pq)]
    for d in range(1, gx_n):
        greet(gx=lax.rem(gx + d, gx_n))
    for d in (1, gy_n - 1):
        greet(gy=lax.rem(gy + d, gy_n))

    @pl.when(gy == 0)
    def _():
        for k in range(1, gy_n):
            greet(gy=k)
            greet(gy=k, gz=0)

        @pl.when(gz != 0)
        def _():
            greet(gz=0)

    kind = jnp.where(gy == 0, 0, jnp.where(gy == gy_n - 1, 2, 1))
    rest = [
        load(2, closure_h, closure), load(3, owner_h, owner), load(4, wall_h.at[gy], wall),
        load(5, ends_h, ends), load(6, patch_h.at[gx], patch), load(7, inner_h, inner),
        load(8, sides_h.at[kind], sides), load(9, fun_h, fun), load(10, val_h.at[kind], val),
        load(11, local_h.at[gx], local), load(13, mix_h.at[gx], mix),
        load(14, blow_h, blow),
    ]

    for copy in first:
        copy.wait()
    for c in range(3):
        pair = dot(pq[...], cot[c * nz * ny : (c + 1) * nz * ny, :])
        pq_out[c, 0] = pair[:nz]
        pq_out[c, 1] = pair[nz:]

    for copy in rest:
        copy.wait()
    deltas = []
    for side in (0, 1):
        deltas.append(ALPHA - (0.5 * ALPHA) * closure[side].astype(F32))
    delta0, delta1 = deltas
    tau, eps = float(cst["t_inv"][0, 1]), float(cst["t_inv"][0, big_y - 2])

    def ends_of(y0, y1, d0, d1):
        p0, p1 = 1.0 - tau * d0, 1.0 - tau * d1
        scale = 1.0 / (p0 * p1 - (eps * eps) * (d0 * d1))
        return (p1 * y0 + eps * (d1 * y1)) * scale, (p0 * y1 + eps * (d0 * y0)) * scale

    lane = lax.broadcasted_iota(jnp.int32, (8, 128), 1)
    row = lax.broadcasted_iota(jnp.int32, (8, 128), 0)

    def wall_copy(z):
        return pltpu.make_async_remote_copy(
            src_ref=w_out.at[0:5], dst_ref=w_in.at[gy, 0:5], send_sem=send_sem.at[5 + z], recv_sem=recv_sem.at[3],
            device_id={"gy": 0, "gz": z}, device_id_type=MESH)

    @pl.when(gz == 0)
    def _():
        blend = sum(blow[c] * cot[c * nz * ny : c * nz * ny + ny, :] for c in range(3))
        parts = dot(wall[...], blend)
        x0, x1 = ends_of(parts[4:5], parts[5:6], delta0[0:1], delta1[0:1])
        parts = parts + ends[0] * (delta0[0:1] * x0) + ends[1] * (delta1[0:1] * x1)
        spread = dot(parts, patch[...])
        total = jnp.zeros((8, 128), F32)
        for q in range(4):
            total += jnp.where((lane // 32 == q) & (row < 4), spread[8 * q : 8 * q + 8], 0.0)
        at = (row == 4) & (lane // 32 == lax.rem(gy, 4))
        for q in range(nx // PATCH):
            owned = owner[0:1, q * PATCH : q * PATCH + 1].astype(F32)
            total += jnp.where(at & (lane % 32 == gx * (nx // PATCH) + q), owned, 0.0)
        w_out[...] = total

    n_wait = (gx_n - 1) + 2 + (gy != 0).astype(jnp.int32)
    n_wait += jnp.where(gz == 0, gz_n - (gy == 0).astype(jnp.int32), 0)
    pl.semaphore_wait(barrier, n_wait)

    @pl.when(gz == 0)
    def _():
        for z in range(gz_n):
            if z == 0:
                @pl.when(gy != 0)
                def _():
                    wall_copy(0).start()

                @pl.when(gy == 0)
                def _():
                    w_in[0] = w_out[...]
            else:
                wall_copy(z).start()

    def pq_copy():
        return pltpu.make_async_remote_copy(
            src_ref=pq_out, dst_ref=pq_in.at[gy], send_sem=send_sem.at[0], recv_sem=recv_sem.at[0],
            device_id={"gy": 0}, device_id_type=MESH)

    @pl.when(gy != 0)
    def _():
        pq_copy().start()

    @pl.when(gy == 0)
    def _():
        pq_in[0] = pq_out[...]

    for c in range(3):
        own[c * nz * ny : (c + 1) * nz * ny, :] = dot(inner[...], cot[c * nz * ny : (c + 1) * nz * ny, :])

    for r in range(4):
        for c in range(3):
            base = c * nz * ny
            halo_out[0, r, c * nz : (c + 1) * nz] = cot[pl.ds(base + ny - 4 + r, nz, stride=ny), :]
            halo_out[1, r, c * nz : (c + 1) * nz] = cot[pl.ds(base + r, nz, stride=ny), :]

    def halo_copy(side):
        return pltpu.make_async_remote_copy(
            src_ref=halo_out.at[side], dst_ref=halo_in.at[side], send_sem=send_sem.at[3 + side],
            recv_sem=recv_sem.at[1 + side],
            device_id={"gy": lax.rem(gy + (1 if side == 0 else gy_n - 1), gy_n)}, device_id_type=MESH)

    for side in (0, 1):
        halo_copy(side).start()

    def v_copy(k):
        return pltpu.make_async_remote_copy(
            src_ref=v_out.at[k], dst_ref=v_in, send_sem=send_sem.at[9], recv_sem=recv_sem.at[6],
            device_id={"gy": k}, device_id_type=MESH)

    root, amp, t_inv = cst["root"], cst["amp"], cst["t_inv"]

    @pl.when(gy == 0)
    def _():
        pltpu.make_async_remote_copy(
            src_ref=pq_in.at[1:gy_n], dst_ref=pq_in.at[1:gy_n], send_sem=send_sem.at[0],
            recv_sem=recv_sem.at[0], device_id={"gy": 0}, device_id_type=MESH).wait_recv()
        hop = float(root**ny)
        far = float(root ** (big_y + 1))
        norm = -amp / (1.0 - far * far)
        sums = []
        for c in range(3):
            before, after = [None] * gy_n, [None] * gy_n
            run = jnp.zeros((nz, nx), F32)
            for m in range(gy_n):
                before[m] = run
                run = hop * run + pq_in[m, c, 0]
            p_all = run
            run = jnp.zeros((nz, nx), F32)
            for m in reversed(range(gy_n)):
                after[m] = run
                run = hop * run + pq_in[m, c, 1]
            q_all = run
            a = float(norm * root) * (q_all - far * p_all)
            b = float(norm * root) * (p_all - far * q_all)
            y0 = float(amp) * q_all + float(root) * a + float(root**big_y) * b
            y1 = float(amp) * p_all + float(root**big_y) * a + float(root) * b
            sums.append((before, after, a, b) + ends_of(y0, y1, delta0, delta1))
        for k in range(gy_n):
            for c in range(3):
                before, after, a, b, x0, x1 = sums[c]

                def at(i, value):
                    value = float(amp) * value + float(root ** (i + 1)) * a + float(root ** (big_y - i)) * b
                    return value + float(t_inv[i, 1]) * (delta0 * x0) + float(t_inv[i, big_y - 2]) * (delta1 * x1)

                low = x0 if k == 0 else at(k * ny - 1, before[k] + float(root) * (hop * after[k] + pq_in[k, c, 1]))
                high = x1 if k == gy_n - 1 else at(
                    (k + 1) * ny, float(root) * (hop * before[k] + pq_in[k, c, 0]) + after[k])
                if k == 0:
                    v_in[c, 0], v_in[c, 1] = low, high
                else:
                    v_out[k, c, 0], v_out[k, c, 1] = low, high
            if k:
                v_copy(k).start()

    def sum_copy(d):
        return pltpu.make_async_remote_copy(
            src_ref=tot_in, dst_ref=sum_in.at[gx], send_sem=send_sem.at[12], recv_sem=recv_sem.at[7],
            device_id={"gx": lax.rem(gx + d, gx_n)}, device_id_type=MESH)

    def tot_copy(k):
        return pltpu.make_async_remote_copy(
            src_ref=tot_out, dst_ref=tot_in, send_sem=send_sem.at[10], recv_sem=recv_sem.at[4],
            device_id={"gy": k}, device_id_type=MESH)

    @pl.when(gy == 0)
    def _():
        @pl.when(gz == 0)
        def _():
            pltpu.make_async_remote_copy(
                src_ref=w_in.at[1:gy_n, 0:5], dst_ref=w_in.at[1:gy_n, 0:5], send_sem=send_sem.at[5],
                recv_sem=recv_sem.at[3], device_id={"gy": 0}, device_id_type=MESH).wait_recv()

        @pl.when(gz != 0)
        def _():
            pltpu.make_async_remote_copy(
                src_ref=w_in.at[:, 0:5], dst_ref=w_in.at[:, 0:5], send_sem=send_sem.at[5],
                recv_sem=recv_sem.at[3], device_id={"gy": 0}, device_id_type=MESH).wait_recv()
        total = jnp.zeros((8, 128), F32)
        for q in range(gy_n // 4):
            group = w_in[4 * q]
            for m in range(4 * q + 1, 4 * q + 4):
                group = group + w_in[m]
            total = total + jnp.where(row < 4, group, 0.0)
            total = total + pltpu.roll(jnp.where(row == 4, group, 0.0), q, 0)
        tot_out[...] = total
        tot_in[...] = total
        for k in range(1, gy_n):
            tot_copy(k).start()
        for d in range(1, gx_n):
            sum_copy(d).start()
        sum_in[gx] = tot_in[...]

    for side in (0, 1):
        halo_copy(side).wait_recv()
    same_row = (
        lax.broadcasted_iota(jnp.int32, (nz * ny, 128), 0) % ny
        == lax.broadcasted_iota(jnp.int32, (nz * ny, 128), 1) % ny
    )
    plane_of = (
        lax.broadcasted_iota(jnp.int32, (nz, nz * ny), 1) // ny
        == lax.broadcasted_iota(jnp.int32, (nz, nz * ny), 0)
    ).astype(F32)
    for c in range(3):
        rows = halo_in[:, :, c * nz : (c + 1) * nz, :].reshape(8 * nz, nx)
        u_c = own[c * nz * ny : (c + 1) * nz * ny, :] + dot(sides[:, : 8 * nz], rows)
        own[c * nz * ny : (c + 1) * nz * ny, :] = u_c
        x_out[c * nz : (c + 1) * nz] = dot(plane_of, jnp.where(same_row, dot(u_c, fun[...]), 0.0))

    @pl.when(gy != 0)
    def _():
        v_copy(0).wait_recv()

    v_rows = []
    for c in range(3):
        low, high = v_in[c, 0], v_in[c, 1]
        v_rows.append([low, high, delta0 * low, delta1 * high])
    sent = [jnp.concatenate([v_rows[c][q] for c in range(3)], axis=0) for q in range(4)]
    sent = jnp.concatenate(sent, axis=1)
    high = sent.astype(jnp.bfloat16)
    low = (sent - high.astype(F32)).astype(jnp.bfloat16)
    pieces = jnp.dot(jnp.concatenate([high, low], axis=0), val[...], preferred_element_type=F32)
    x_out[...] += pieces[:planes, :128] + (pieces[planes:, :128] + pieces[:planes, 128:])


    def x_copy(d):
        return pltpu.make_async_remote_copy(
            src_ref=x_out, dst_ref=x_in.at[gx], send_sem=send_sem.at[11], recv_sem=recv_sem.at[5],
            device_id={"gx": lax.rem(gx + d, gx_n)}, device_id_type=MESH)

    for d in range(1, gx_n):
        x_copy(d).start()
    x_in[gx] = x_out[...]

    @pl.when(gy != 0)
    def _():
        tot_copy(0).wait_recv()
        for d in range(1, gx_n):
            sum_copy(d).start()
        sum_in[gx] = tot_in[...]

    stores = []
    for c in range(3):
        part = pl.ds(c * nz * ny, nz * ny)
        u_c = own[part, :] + dot(sides[:, 8 * nz :], jnp.concatenate(v_rows[c], axis=0))
        own[part, :] = dot(u_c, local[...])
        stores.append(pltpu.make_async_copy(own.at[part, :], grad_o.at[part, :], load_sem.at[c]))
        stores[-1].start()

    pltpu.make_async_remote_copy(
        src_ref=x_in.at[0 : gx_n - 1], dst_ref=x_in.at[0 : gx_n - 1], send_sem=send_sem.at[11],
        recv_sem=recv_sem.at[5], device_id={"gx": 0}, device_id_type=MESH).wait_recv()
    for c in range(3):
        value, to_r, to_p = (jnp.zeros((nz, 128), F32) for _ in range(3))
        for m in range(gx_n):
            part = x_in[m, c * nz : (c + 1) * nz]
            value += mix[m, 0:1] * part
            to_r += mix[m, 1:2] * part
            to_p += mix[m, 2:3] * part
        small_o[c * nz : (c + 1) * nz] = value + pltpu.roll(to_r, ny, 1) + pltpu.roll(to_p, 128 - ny, 1)
    pltpu.make_async_remote_copy(
        src_ref=sum_in.at[0 : gx_n - 1], dst_ref=sum_in.at[0 : gx_n - 1], send_sem=send_sem.at[12],
        recv_sem=recv_sem.at[7], device_id={"gx": 0}, device_id_type=MESH).wait_recv()
    total = sum_in[0]
    for m in range(1, gx_n):
        total = total + sum_in[m]
    mine = ((gx * gy_n + gy) * gz_n + gz).astype(F32)
    hit = (pltpu.roll(total, 4, 0) == mine) & (row < gy_n // 4) & (lane % 32 < gx_n * nx // PATCH)
    small_o[planes : planes + 8] = jnp.where(hit, total, 0.0)

    for copy in stores:
        copy.wait()

    @pl.when(gy != 0)
    def _():
        pq_copy().wait_send()

    for side in (0, 1):
        halo_copy(side).wait_send()

    @pl.when(gz == 0)
    def _():
        for z in range(1, gz_n):
            wall_copy(z).wait_send()

        @pl.when(gy != 0)
        def _():
            wall_copy(0).wait_send()

    @pl.when(gy == 0)
    def _():
        pltpu.make_async_remote_copy(
            src_ref=v_out.at[1:gy_n], dst_ref=v_out.at[1:gy_n], send_sem=send_sem.at[9],
            recv_sem=recv_sem.at[6], device_id={"gy": 0}, device_id_type=MESH).wait_send()
        for k in range(1, gy_n):
            tot_copy(k).wait_send()

    for d in range(1, gx_n):
        x_copy(d).wait_send()
        sum_copy(d).wait_send()


def finish(sizes, part_h, small_h, shapes_h, grad_h, act_h, part, small, shapes, act, sem):
    gx_n, gy_n, gz_n, ny, nx, nz = sizes
    block = nz * ny
    loads = [
        pltpu.make_async_copy(small_h, small, sem.at[3]),
        pltpu.make_async_copy(shapes_h.at[lax.axis_index("gx")], shapes, sem.at[4]),
    ] + [
        pltpu.make_async_copy(part_h.at[pl.ds(c * block, block), :], part.at[pl.ds(c * block, block), :], sem.at[c])
        for c in range(3)
    ]
    for copy in loads:
        copy.start()
    same_row = (
        lax.broadcasted_iota(jnp.int32, (block, 128), 0) % ny
        == lax.broadcasted_iota(jnp.int32, (block, 128), 1) % ny
    )
    loads[0].wait()
    loads[1].wait()
    act[...] = jnp.sum(small[3 * nz :], keepdims=True)
    stores = [pltpu.make_async_copy(act, act_h, sem.at[8])]
    stores[0].start()
    for c in range(3):
        value = small[c * nz : (c + 1) * nz]
        high = value.astype(jnp.bfloat16).astype(F32)
        spread = [
            jnp.where(same_row, jnp.broadcast_to(v[:, None, :], (nz, ny, 128)).reshape(block, 128), 0.0)
            for v in (high, value - high)
        ]
        both = jnp.concatenate(spread, axis=1).astype(jnp.bfloat16)
        added = jnp.dot(both, shapes[...], preferred_element_type=F32)
        added = added[:, :nx] + added[:, nx:]
        loads[2 + c].wait()
        part[c * block : (c + 1) * block, :] += added
        stores.append(
            pltpu.make_async_copy(part.at[pl.ds(c * block, block), :], grad_h.at[pl.ds(c * block, block), :], sem.at[5 + c])
        )
        stores[-1].start()
    for copy in stores:
        copy.wait()


def on_device(sizes, cst, cotangent, closure, owner, blowing):
    gx_n, gy_n, gz_n, ny, nx, nz = sizes
    f32 = lambda name: jnp.asarray(np.asarray(cst[name], np.float32))

    def halves(name, axis):
        exact = np.asarray(cst[name], np.float32)
        high = exact.astype(jnp.bfloat16)
        low = (exact - high.astype(np.float32)).astype(jnp.bfloat16)
        return np.concatenate([high, low], axis=axis)

    names = ("inner", "pq", "sides", "fun", "val", "local", "mix", "wall", "ends", "patch")
    tables = [jnp.asarray(halves(n, 2)) if n == "val" else f32(n) for n in names]
    anyspec = pl.BlockSpec(memory_space=pltpu.HBM)
    vmem = pl.BlockSpec(memory_space=pltpu.VMEM)
    v = lambda *shape: pltpu.VMEM(shape, F32)
    rows = 3 * nz * ny
    scratch = [
        v(rows, nx), pltpu.VMEM((2, nz, nx), jnp.int32), pltpu.VMEM((ny, nx), jnp.int32), pltpu.SMEM((3,), F32),
        v(nz * ny, nz * ny), v(2 * nz, nz * ny), v(nz * ny, 12 * nz), v(nx, 128), pltpu.VMEM((4 * nx, 256), jnp.bfloat16),
        v(nx, nx), v(gx_n, 4, 128), v(32, ny), v(2, 32, 128), v(nx, 128),
        v(3, 2, nz, nx), v(gy_n, 3, 2, nz, nx), v(2, 4, 3 * nz, nx), v(2, 4, 3 * nz, nx),
        v(gy_n, 3, 2, nz, nx), v(3, 2, nz, nx), v(8, 128), v(gy_n, 8, 128), v(8, 128), v(8, 128),
        v(3 * nz, 128), v(gx_n, 3 * nz, 128), v(gx_n, 8, 128), v(rows, nx),
        pltpu.SemaphoreType.DMA((15,)), pltpu.SemaphoreType.DMA((13,)), pltpu.SemaphoreType.DMA((8,)),
    ]
    part, small = pl.pallas_call(
        functools.partial(kernel, sizes, cst),
        out_shape=(jax.ShapeDtypeStruct((rows, nx), F32), jax.ShapeDtypeStruct((3 * nz + 8, 128), F32)),
        in_specs=[anyspec] * (4 + len(tables)),
        out_specs=(anyspec, vmem),
        scratch_shapes=scratch,
        compiler_params=pltpu.CompilerParams(
            collective_id=0, has_side_effects=True, vmem_limit_bytes=64 * 1024 * 1024
        ),
    )(cotangent.reshape(rows, nx), jnp.transpose(closure, (0, 2, 1)), owner.T, blowing, *tables)
    shapes = jnp.asarray(np.tile(halves("shapes", 2), (1, 2, 1)))
    gradient, share = pl.pallas_call(
        functools.partial(finish, sizes),
        out_shape=(jax.ShapeDtypeStruct((rows, nx), F32), jax.ShapeDtypeStruct((1, 1), F32)),
        in_specs=[anyspec] * 3,
        out_specs=(anyspec, anyspec),
        scratch_shapes=[
            v(rows, nx), v(3 * nz + 8, 128), pltpu.VMEM((256, 2 * nx), jnp.bfloat16), v(1, 1), pltpu.SemaphoreType.DMA((9,)),
        ],
        compiler_params=pltpu.CompilerParams(vmem_limit_bytes=64 * 1024 * 1024),
    )(part, small, shapes)
    return gradient.reshape(cotangent.shape), share.reshape(1)


def solution(mesh):
    gx_n, gy_n, gz_n = (mesh.shape[a] for a in ("gx", "gy", "gz"))
    sizes = (gx_n, gy_n, gz_n, 512 // 16, 1024 // 8, 32 // 4)
    cst = constants(gx_n, gy_n, sizes[3], sizes[4], sizes[5])
    in_specs = (P(None, "gz", "gy", "gx"), P(None, "gx", "gz"), P("gx", "gy"), P())
    out_specs = (P(None, "gz", "gy", "gx"), P(("gx", "gy", "gz")))
    return jax.shard_map(
        functools.partial(on_device, sizes, cst),
        mesh=mesh, in_specs=in_specs, out_specs=out_specs, check_vma=False,
    )
```
